32 devices in a mesh: wide: 8 (over y, x, core), narrow: 4 (over z).
Axes of the slice: x: 2, y: 2, z: 4, core: 2. Of those that a mesh axis runs over, the one named last changes fastest.
Arguments:
- sources: int32 [256, 256, 256], P('wide', 'narrow'), may hold values from 0 to 1
- labels: int32 [256, 256, 256], P('wide', 'narrow'), may hold values from 0 to 1, as said below
Outputs:
- distance: float32 [256, 256, 256], P('wide', 'narrow')
The draws below stay inside these ranges and needn't reach their ends.
Inputs may be any that keep to these rules, and one draw needn't show every extreme that they name: labels marks the union of several periodic balls of radii between 16 and 42 cells; sources marks exactly the labelled cells that have an unlabelled neighbour along one of the six grid directions.
All inputs are finite; a program needn't handle non-finite values.
Results may differ from the reference program's by a relative error of at most 0.00022.
Values sent between devices are 32-bit elements; how exact they have to be, the bound alone decides.
A program may use at most 128 MiB of HBM per device.

```python
import math
import jax
import jax.numpy as jnp

G = 256


def ball_union(key):
    inner = jax.random.fold_in(key, 7)
    key_centers, key_radii = jax.random.split(inner)
    centers = jax.random.randint(key_centers, (8, 3), 0, G, dtype=jnp.int32)
    radii = jax.random.randint(key_radii, (8,), G // 16, G // 6 + 1, dtype=jnp.int32)
    positions = jnp.arange(G, dtype=jnp.int32)
    inside = jnp.zeros((G, G, G), dtype=jnp.bool_)
    for ball in range(8):
        offset_x = (positions - centers[ball, 0] + G // 2) % G - G // 2
        offset_y = (positions - centers[ball, 1] + G // 2) % G - G // 2
        offset_z = (positions - centers[ball, 2] + G // 2) % G - G // 2
        square = (offset_x * offset_x)[:, None, None] + (offset_y * offset_y)[None, :, None] + (offset_z * offset_z)[None, None, :]
        inside = inside | (square <= radii[ball] * radii[ball])
    return inside


def draw_labels(key, part):
    return ball_union(key).astype(jnp.int32)


def draw_sources(key, part):
    inside = ball_union(key)
    outside_near = jnp.zeros_like(inside)
    for dimension in range(3):
        outside_near = outside_near | jnp.logical_not(jnp.roll(inside, 1, dimension))
        outside_near = outside_near | jnp.logical_not(jnp.roll(inside, -1, dimension))
    return (inside & outside_near).astype(jnp.int32)


def setup_inputs(seed: int = 0) -> dict:
    arg_keys = jax.random.split(jax.random.key(seed), 3)
    return {
        "sources": draw_sources(jax.random.fold_in(arg_keys[2], 71), 0),
        "labels": draw_labels(jax.random.fold_in(arg_keys[2], 71), 0),
    }


def wave_terms(length):
    positions = jnp.arange(length, dtype=jnp.int32).astype(jnp.float32)
    angles = positions * (2.0 * math.pi / length)
    return (2.0 - 2.0 * jnp.cos(angles), jnp.sin(angles))

def central(values, dimension):
    return 0.5 * (jnp.roll(values, -1, dimension) - jnp.roll(values, 1, dimension))

def reference(sources, labels):
    heat_time = (G / 8.0) ** 2
    grad_floor = 0.04 / heat_time
    source = sources.astype(jnp.float32)
    eigenvalue, sine_wave = wave_terms(G)
    laplace = eigenvalue[:, None, None] + eigenvalue[None, :, None] + eigenvalue[None, None, :]
    spectrum = jnp.fft.fftn(source)
    heat_field = jnp.real(jnp.fft.ifftn(spectrum / (1.0 + heat_time * laplace))).astype(jnp.float32)
    grad_x = central(heat_field, 0)
    grad_y = central(heat_field, 1)
    grad_z = central(heat_field, 2)
    magnitude = jnp.sqrt(grad_x * grad_x + grad_y * grad_y + grad_z * grad_z)
    limited = jnp.maximum(magnitude, grad_floor)
    flow_x = -grad_x / limited
    flow_y = -grad_y / limited
    flow_z = -grad_z / limited
    divergence = central(flow_x, 0) + central(flow_y, 1) + central(flow_z, 2)
    laplace_safe = laplace.at[0, 0, 0].set(1.0)
    potential_hat = -jnp.fft.fftn(divergence) / laplace_safe
    potential_hat = potential_hat.at[0, 0, 0].set(0.0)
    potential = jnp.real(jnp.fft.ifftn(potential_hat)).astype(jnp.float32)
    signs = (2 * labels - 1).astype(jnp.float32)
    return signs * potential
```

```python
from functools import partial
import math

import jax
import jax.numpy as jnp
from jax import lax
from jax.experimental import pallas as pl
from jax.experimental.pallas import tpu as pltpu
from jax.sharding import PartitionSpec as P
import numpy as np

highest = lax.Precision.HIGHEST
moment_rows = 8


def cas_table(length):
    positions = np.arange(length)
    angles = (positions[:, None] * positions[None, :] % length) * (2.0 * math.pi / length)
    return (np.cos(angles) + np.sin(angles)).astype(np.float32)


def decay_table(length, shift):
    eigen = 4.0 * np.sin(np.pi * np.arange(length) / length) ** 2
    lam = shift + eigen[:, None] + eigen[None, :]
    return np.where(lam > 0.0, np.exp(-2.0 * np.arcsinh(0.5 * np.sqrt(lam))), 0.0).astype(np.float32)


def column_tables(length, blocks):
    span = length // blocks
    const = (length * length - 1.0) / (12.0 * length)
    j = np.arange(span, dtype=np.float64)
    gap = np.abs(j[:, None] - j[None, :])
    parts = [gap * (gap - length) / (2.0 * length) + const]
    centred = j - (span - 1) / 2.0
    for delta in range(1, blocks):
        a = centred + length - span * delta
        rows = np.zeros((span, moment_rows))
        rows[:, 0] = (a * a - length * a) / (2.0 * length) + const
        rows[:, 1] = -(2.0 * a - length) / (2.0 * length)
        rows[:, 2] = 1.0 / (2.0 * length)
        parts.append(rows)
    moments = np.zeros((moment_rows, span))
    moments[0], moments[1], moments[2] = 1.0, centred, centred * centred
    return np.concatenate(parts, axis=1).astype(np.float32), moments.astype(np.float32)


def power(base, exponent):
    result = None
    while exponent:
        if exponent & 1:
            result = base if result is None else result * base
        base = base * base
        exponent >>= 1
    return result


def solve_kernel(n, field, table, decay, scale, green, moments, mask, out, work, sent, arrived, send_sem, recv_sem):
    span, layers, length = work.shape
    lanes = 128
    group = lanes // layers
    chunks = span // group
    me = lax.axis_index("narrow")
    barrier = pltpu.get_barrier_semaphore()
    for step in range(1, n):
        pl.semaphore_signal(
            barrier, inc=1, device_id={"narrow": lax.rem(me + step, n)}, device_id_type=pl.DeviceIdType.MESH
        )

    def to_waves(c, carry):
        columns = pl.ds(pl.multiple_of(c * lanes, lanes), lanes)
        block = lax.dot_general(
            field[:, columns].T, table[...], (((1,), (0,)), ((), ())), precision=highest,
            preferred_element_type=jnp.float32,
        )
        work[pl.ds(c * group, group)] = block.reshape(group, layers, length)
        return carry

    lax.fori_loop(0, chunks, to_waves, 0)
    r = decay[...]
    s = scale[...]
    column = work[:, 0, :]
    sent[2 * layers :, :] = jnp.dot(moments[...], column, precision=highest, preferred_element_type=jnp.float32)

    def ahead(j, v):
        v = work[j] + r * v
        work[j] = v
        return v

    v_last = lax.fori_loop(0, span, ahead, jnp.zeros_like(r), unroll=4)

    def back(i, u):
        j = span - 1 - i
        u = s * work[j] + r * u
        work[j] = u
        return u

    u_first = lax.fori_loop(0, span, back, jnp.zeros_like(r), unroll=4)
    sent[0:layers, :] = v_last
    sent[layers : 2 * layers, :] = u_first
    pl.semaphore_wait(barrier, n - 1)
    copies = []
    for step in range(1, n):
        copy = pltpu.make_async_remote_copy(
            src_ref=sent,
            dst_ref=arrived.at[n - 1 - step],
            send_sem=send_sem.at[step - 1],
            recv_sem=recv_sem.at[n - 1 - step],
            device_id={"narrow": lax.rem(me + step, n)},
            device_id_type=pl.DeviceIdType.MESH,
        )
        copy.start()
        copies.append(copy)
    for copy in copies:
        copy.wait()
    stacked = jnp.concatenate([column] + [arrived[d, 2 * layers :, :] for d in range(n - 1)], axis=0)
    extra = jnp.dot(green[...], stacked, precision=highest, preferred_element_type=jnp.float32) * mask[...]
    last = [v_last] + [arrived[d, 0:layers, :] for d in range(n - 1)]
    first = [u_first] + [arrived[d, layers : 2 * layers, :] for d in range(n - 1)]
    q = power(r, span)
    close = 1.0 / (1.0 - power(q, n))
    factor = s / (1.0 - r * r)
    tail = q * r
    edge = r - tail * q
    alphas = []
    for t in range(n):
        total = last[t % n]
        for k in range(n - 2, -1, -1):
            total = last[(t - 1 - k) % n] + q * total
        alphas.append(total * close * factor)
    begin = [first[t] + alphas[t] * edge for t in range(n)]
    total = begin[0]
    for k in range(n - 2, -1, -1):
        total = begin[(1 + k) % n] + q * total
    inflow = total * close

    def add_ahead(j, p):
        work[j] = work[j] + p
        return p * r

    lax.fori_loop(0, span, add_ahead, alphas[0] * r, unroll=4)

    def add_back(i, p):
        j = span - 1 - i
        work[j] = work[j] + p
        return p * r

    lax.fori_loop(0, span, add_back, (inflow - alphas[0] * tail) * r, unroll=4)
    work[:, 0, :] = work[:, 0, :] + extra

    def from_waves(c, carry):
        columns = pl.ds(pl.multiple_of(c * lanes, lanes), lanes)
        block = work[pl.ds(c * group, group)].reshape(lanes, length)
        out[:, columns] = lax.dot_general(
            table[...], block, (((1,), (1,)), ((), ())), precision=highest, preferred_element_type=jnp.float32
        )
        return carry

    lax.fori_loop(0, chunks, from_waves, 0)


def solve_lines(field, tables, decay, scale, mask, layers):
    length, columns = field.shape
    n = lax.axis_size("narrow")
    span = columns // layers
    rows = 2 * layers + moment_rows
    vmem = pl.BlockSpec(memory_space=pltpu.VMEM)
    return pl.pallas_call(
        partial(solve_kernel, n),
        out_shape=jax.ShapeDtypeStruct((length, columns), jnp.float32),
        in_specs=[vmem] * 7,
        out_specs=vmem,
        scratch_shapes=[
            pltpu.VMEM((span, layers, length), jnp.float32),
            pltpu.VMEM((rows, length), jnp.float32),
            pltpu.VMEM((n - 1, rows, length), jnp.float32),
            pltpu.SemaphoreType.DMA((n - 1,)),
            pltpu.SemaphoreType.DMA((n - 1,)),
        ],
        compiler_params=pltpu.CompilerParams(
            collective_id=0, has_side_effects=True, vmem_limit_bytes=40 * 1024 * 1024
        ),
        cost_estimate=pl.CostEstimate(
            flops=4 * length * length * columns, bytes_accessed=8 * length * columns, transcendentals=0
        ),
        name="lines",
    )(field, tables[0], decay, scale, tables[1], tables[2], mask)


def solve(real_field, tables, decay, scale, mask):
    table = tables[0]
    span_wide, span_narrow, length = real_field.shape
    wide = lax.axis_size("wide")
    layers = length // wide
    waves = jnp.einsum("xyz,zk->xyk", real_field, table, precision=highest)
    blocks = waves.reshape(span_wide, span_narrow, wide, layers).transpose(2, 0, 1, 3)
    arrived = lax.all_to_all(
        blocks.reshape(wide, span_wide, span_narrow * layers), "wide", split_axis=0, concat_axis=0, tiled=True
    )
    lines = solve_lines(arrived.reshape(length, span_narrow * layers), tables, decay, scale, mask, layers)
    returned = lax.all_to_all(
        lines.reshape(wide, span_wide, span_narrow * layers), "wide", split_axis=0, concat_axis=0, tiled=True
    )
    waves = returned.reshape(wide, span_wide, span_narrow, layers).transpose(1, 2, 0, 3)
    return jnp.einsum("xyk,kz->xyz", waves.reshape(span_wide, span_narrow, length), table, precision=highest)


def extended(x, sides, width):
    for axis, dim in sides:
        peers, length = (lax.axis_size(axis), x.shape[dim])
        up = [(i, (i + 1) % peers) for i in range(peers)]
        down = [(j, i) for i, j in up]
        last = lax.slice_in_dim(x, length - width, length, axis=dim)
        initial = lax.slice_in_dim(x, 0, width, axis=dim)
        before = lax.ppermute(last, axis, up)
        after = lax.ppermute(initial, axis, down)
        x = jnp.concatenate([before, x, after], axis=dim)
    return x


def central_last(values):
    return 0.5 * (jnp.roll(values, -1, values.ndim - 1) - jnp.roll(values, 1, values.ndim - 1))


def flow_divergence(heat_field, grad_floor):
    padded = extended(heat_field, (("wide", 0), ("narrow", 1)), 2)
    grad_x = 0.5 * (padded[2:, 1:-1] - padded[:-2, 1:-1])
    grad_y = 0.5 * (padded[1:-1, 2:] - padded[1:-1, :-2])
    grad_z = central_last(padded[1:-1, 1:-1])
    magnitude = jnp.sqrt(grad_x * grad_x + grad_y * grad_y + grad_z * grad_z)
    inverse = -1.0 / jnp.maximum(magnitude, grad_floor)
    flow_x = grad_x * inverse
    flow_y = grad_y * inverse
    flow_z = (grad_z * inverse)[1:-1, 1:-1]
    return (
        0.5 * (flow_x[2:, 1:-1] - flow_x[:-2, 1:-1])
        + 0.5 * (flow_y[1:-1, 2:] - flow_y[1:-1, :-2])
        + central_last(flow_z)
    )


def per_device(sources, labels):
    length = sources.shape[2]
    heat_time = (length / 8.0) ** 2
    grad_floor = 0.04 / heat_time
    wide = lax.axis_size("wide")
    layers = length // wide
    place = lax.axis_index("wide")
    green, moments = column_tables(length, lax.axis_size("narrow"))
    tables = (jnp.asarray(cas_table(length)), jnp.asarray(green), jnp.asarray(moments))

    def mine(table):
        return lax.dynamic_slice_in_dim(jnp.asarray(table), place * layers, layers, axis=0)

    heat_decay = mine(decay_table(length, 1.0 / heat_time))
    line_decay = mine(decay_table(length, 0.0))
    corner = (jnp.arange(length, dtype=jnp.int32)[None, :] == 0) & (place == 0)
    norm = float(length) ** 2
    heat_field = solve(
        sources.astype(jnp.float32), tables, heat_decay, heat_decay * (1.0 / (heat_time * norm)),
        jnp.zeros((1, length), jnp.float32),
    )
    divergence = flow_divergence(heat_field, grad_floor)
    potential = solve(
        divergence, tables, line_decay, line_decay * (-1.0 / norm), jnp.where(corner, -1.0 / norm, 0.0)
    )
    signs = (2 * labels - 1).astype(jnp.float32)
    return signs * potential


def solution(mesh):
    return jax.shard_map(
        per_device,
        mesh=mesh,
        in_specs=(P("wide", "narrow", None), P("wide", "narrow", None)),
        out_specs=P("wide", "narrow", None),
        check_vma=False,
    )
```

```python
from functools import partial
import math

import jax
import jax.numpy as jnp
from jax import lax
from jax.experimental import pallas as pl
from jax.experimental.pallas import tpu as pltpu
from jax.sharding import PartitionSpec as P
import numpy as np

highest = lax.Precision.HIGHEST
moment_rows = 8
lanes = 128


def cas_table(length):
    positions = np.arange(length)
    angles = (positions[:, None] * positions[None, :] % length) * (2.0 * math.pi / length)
    return (np.cos(angles) + np.sin(angles)).astype(np.float32)


def decay_table(length, shift):
    eigen = 4.0 * np.sin(np.pi * np.arange(length) / length) ** 2
    lam = shift + eigen[:, None] + eigen[None, :]
    return np.where(lam > 0.0, np.exp(-2.0 * np.arcsinh(0.5 * np.sqrt(lam))), 0.0).astype(np.float32)


def column_tables(length, blocks):
    span = length // blocks
    const = (length * length - 1.0) / (12.0 * length)
    j = np.arange(span, dtype=np.float64)
    gap = np.abs(j[:, None] - j[None, :])
    parts = [gap * (gap - length) / (2.0 * length) + const]
    centred = j - (span - 1) / 2.0
    for delta in range(1, blocks):
        a = centred + length - span * delta
        rows = np.zeros((span, moment_rows))
        rows[:, 0] = (a * a - length * a) / (2.0 * length) + const
        rows[:, 1] = -(2.0 * a - length) / (2.0 * length)
        rows[:, 2] = 1.0 / (2.0 * length)
        parts.append(rows)
    moments = np.zeros((moment_rows, span))
    moments[0], moments[1], moments[2] = 1.0, centred, centred * centred
    return np.concatenate(parts, axis=1).astype(np.float32), moments.astype(np.float32)


def power(base, exponent):
    result = None
    while exponent:
        if exponent & 1:
            result = base if result is None else result * base
        base = base * base
        exponent >>= 1
    return result


def solve_kernel(n, field, table, decay, scale, green, moments, mask, out, work, sent, arrived, send_sem, recv_sem):
    span, layers, length = work.shape
    group = lanes // layers
    chunks = span // group
    me = lax.axis_index("narrow")
    barrier = pltpu.get_barrier_semaphore()
    for step in range(1, n):
        pl.semaphore_signal(
            barrier, inc=1, device_id={"narrow": lax.rem(me + step, n)}, device_id_type=pl.DeviceIdType.MESH
        )

    def to_waves(c, carry):
        block = lax.dot_general(
            field[:, c].reshape(length, lanes).T, table[...], (((1,), (0,)), ((), ())), precision=highest,
            preferred_element_type=jnp.float32,
        )
        work[pl.ds(c * group, group)] = block.reshape(group, layers, length)
        return carry

    lax.fori_loop(0, chunks, to_waves, 0)
    r = decay[...]
    s = scale[...]
    column = work[:, 0, :]
    sent[2 * layers :, :] = jnp.dot(moments[...], column, precision=highest, preferred_element_type=jnp.float32)

    def ahead(j, v):
        v = work[j] + r * v
        work[j] = v
        return v

    v_last = lax.fori_loop(0, span, ahead, jnp.zeros_like(r), unroll=4)

    def back(i, u):
        j = span - 1 - i
        u = s * work[j] + r * u
        work[j] = u
        return u

    u_first = lax.fori_loop(0, span, back, jnp.zeros_like(r), unroll=4)
    sent[0:layers, :] = v_last
    sent[layers : 2 * layers, :] = u_first
    pl.semaphore_wait(barrier, n - 1)
    copies = []
    for step in range(1, n):
        copy = pltpu.make_async_remote_copy(
            src_ref=sent,
            dst_ref=arrived.at[n - 1 - step],
            send_sem=send_sem.at[step - 1],
            recv_sem=recv_sem.at[n - 1 - step],
            device_id={"narrow": lax.rem(me + step, n)},
            device_id_type=pl.DeviceIdType.MESH,
        )
        copy.start()
        copies.append(copy)
    for copy in copies:
        copy.wait()
    stacked = jnp.concatenate([column] + [arrived[d, 2 * layers :, :] for d in range(n - 1)], axis=0)
    extra = jnp.dot(green[...], stacked, precision=highest, preferred_element_type=jnp.float32) * mask[...]
    last = [v_last] + [arrived[d, 0:layers, :] for d in range(n - 1)]
    first = [u_first] + [arrived[d, layers : 2 * layers, :] for d in range(n - 1)]
    q = power(r, span)
    close = 1.0 / (1.0 - power(q, n))
    factor = s / (1.0 - r * r)
    tail = q * r
    edge = r - tail * q
    alphas = []
    for t in range(n):
        total = last[t % n]
        for k in range(n - 2, -1, -1):
            total = last[(t - 1 - k) % n] + q * total
        alphas.append(total * close * factor)
    begin = [first[t] + alphas[t] * edge for t in range(n)]
    total = begin[0]
    for k in range(n - 2, -1, -1):
        total = begin[(1 + k) % n] + q * total
    inflow = total * close

    def add_ahead(j, p):
        work[j] = work[j] + p
        return p * r

    lax.fori_loop(0, span, add_ahead, alphas[0] * r, unroll=4)

    def add_back(i, p):
        j = span - 1 - i
        work[j] = work[j] + p
        return p * r

    lax.fori_loop(0, span, add_back, (inflow - alphas[0] * tail) * r, unroll=4)
    work[:, 0, :] = work[:, 0, :] + extra

    def from_waves(c, carry):
        block = work[pl.ds(c * group, group)].reshape(lanes, length)
        result = lax.dot_general(
            table[...], block, (((1,), (1,)), ((), ())), precision=highest, preferred_element_type=jnp.float32
        )
        out[:, c] = result.reshape(out.shape[0], out.shape[2], lanes)
        return carry

    lax.fori_loop(0, chunks, from_waves, 0)


def solve_lines(field, tables, decay, scale, mask, layers):
    length = field.shape[0] * field.shape[2]
    columns = field.shape[1] * lanes
    n = lax.axis_size("narrow")
    span = columns // layers
    rows = 2 * layers + moment_rows
    vmem = pl.BlockSpec(memory_space=pltpu.VMEM)
    return pl.pallas_call(
        partial(solve_kernel, n),
        out_shape=jax.ShapeDtypeStruct(field.shape, jnp.float32),
        in_specs=[vmem] * 7,
        out_specs=vmem,
        scratch_shapes=[
            pltpu.VMEM((span, layers, length), jnp.float32),
            pltpu.VMEM((rows, length), jnp.float32),
            pltpu.VMEM((n - 1, rows, length), jnp.float32),
            pltpu.SemaphoreType.DMA((n - 1,)),
            pltpu.SemaphoreType.DMA((n - 1,)),
        ],
        compiler_params=pltpu.CompilerParams(
            collective_id=0, has_side_effects=True, vmem_limit_bytes=40 * 1024 * 1024
        ),
        cost_estimate=pl.CostEstimate(
            flops=4 * length * length * columns, bytes_accessed=8 * length * columns, transcendentals=0
        ),
        name="lines",
    )(field, tables[0], decay, scale, tables[1], tables[2], mask)


def split_kernel(field, table, blocks, waves):
    xs, span, length = field.shape
    wide = blocks.shape[0]
    layers = length // wide
    group = lanes // layers
    halves = length // lanes
    step = max(1, 256 // span)

    def transform(c, carry):
        rows = field[pl.ds(c * step, step)].astype(jnp.float32).reshape(step * span, length)
        result = jnp.dot(rows, table[...], precision=highest, preferred_element_type=jnp.float32)
        start = pl.multiple_of(c * step * span, step * span)
        for h in range(halves):
            waves[h, pl.ds(start, step * span), :] = result[:, h * lanes : (h + 1) * lanes]
        return carry

    lax.fori_loop(0, xs // step, transform, 0)
    slot_of = lax.broadcasted_iota(jnp.int32, (xs, lanes), 1) // layers

    def place(g, carry):
        for h in range(halves):
            pieces = [waves[h, pl.ds(g * group + i, xs, stride=span), :] for i in range(group)]
            for slot in range(group):
                total = None
                for i in range(group):
                    shift = ((i - slot) * layers) % lanes
                    moved = pltpu.roll(pieces[i], shift, 1) if shift else pieces[i]
                    total = moved if total is None else jnp.where(slot_of == i, moved, total)
                blocks[h * group + slot, g] = total
        return carry

    lax.fori_loop(0, span // group, place, 0)


def join_kernel(signed, blocks, table, *rest):
    labels = rest[0] if signed else None
    field, waves = rest[-2:]
    xs, span, length = field.shape
    wide = blocks.shape[0]
    layers = length // wide
    group = lanes // layers
    halves = length // lanes
    step = max(1, 256 // span)
    slot_of = lax.broadcasted_iota(jnp.int32, (xs, lanes), 1) // layers

    def place(g, carry):
        for h in range(halves):
            pieces = [blocks[h * group + slot, g] for slot in range(group)]
            for i in range(group):
                total = None
                for slot in range(group):
                    shift = ((slot - i) * layers) % lanes
                    moved = pltpu.roll(pieces[slot], shift, 1) if shift else pieces[slot]
                    total = moved if total is None else jnp.where(slot_of == slot, moved, total)
                waves[h, pl.ds(g * group + i, xs, stride=span), :] = total
        return carry

    lax.fori_loop(0, span // group, place, 0)

    def transform(c, carry):
        start = pl.multiple_of(c * step * span, step * span)
        rows = jnp.concatenate([waves[h, pl.ds(start, step * span), :] for h in range(halves)], axis=1)
        result = jnp.dot(rows, table[...], precision=highest, preferred_element_type=jnp.float32)
        result = result.reshape(step, span, length)
        if signed:
            result = result * (2 * labels[pl.ds(c * step, step)] - 1).astype(jnp.float32)
        field[pl.ds(c * step, step)] = result
        return carry

    lax.fori_loop(0, xs // step, transform, 0)


def local_call(kernel, args, shape, rows, length, name):
    vmem = pl.BlockSpec(memory_space=pltpu.VMEM)
    return pl.pallas_call(
        kernel,
        out_shape=jax.ShapeDtypeStruct(shape, jnp.float32),
        in_specs=[vmem] * len(args),
        out_specs=vmem,
        scratch_shapes=[pltpu.VMEM((length // lanes, rows, lanes), jnp.float32)],
        compiler_params=pltpu.CompilerParams(vmem_limit_bytes=40 * 1024 * 1024),
        cost_estimate=pl.CostEstimate(
            flops=2 * rows * length * length, bytes_accessed=8 * rows * length, transcendentals=0
        ),
        name=name,
    )(*args)


def solve(real_field, tables, decay, scale, mask, labels=None):
    table = tables[0]
    xs, span, length = real_field.shape
    wide = lax.axis_size("wide")
    layers = length // wide
    shape = (wide, span * layers // lanes, xs, lanes)
    blocks = local_call(split_kernel, (real_field, table), shape, xs * span, length, "split")
    blocks = lax.all_to_all(blocks, "wide", split_axis=0, concat_axis=0, tiled=True)
    blocks = solve_lines(blocks, tables, decay, scale, mask, layers)
    blocks = lax.all_to_all(blocks, "wide", split_axis=0, concat_axis=0, tiled=True)
    args = (blocks, table) if labels is None else (blocks, table, labels)
    kernel = partial(join_kernel, labels is not None)
    return local_call(kernel, args, real_field.shape, xs * span, length, "join")


def extended(x, sides, width):
    for axis, dim in sides:
        peers, length = (lax.axis_size(axis), x.shape[dim])
        up = [(i, (i + 1) % peers) for i in range(peers)]
        down = [(j, i) for i, j in up]
        last = lax.slice_in_dim(x, length - width, length, axis=dim)
        initial = lax.slice_in_dim(x, 0, width, axis=dim)
        before = lax.ppermute(last, axis, up)
        after = lax.ppermute(initial, axis, down)
        x = jnp.concatenate([before, x, after], axis=dim)
    return x


def central_last(values):
    return 0.5 * (jnp.roll(values, -1, values.ndim - 1) - jnp.roll(values, 1, values.ndim - 1))


def flow_divergence(heat_field, grad_floor):
    padded = extended(heat_field, (("wide", 0), ("narrow", 1)), 2)
    grad_x = 0.5 * (padded[2:, 1:-1] - padded[:-2, 1:-1])
    grad_y = 0.5 * (padded[1:-1, 2:] - padded[1:-1, :-2])
    grad_z = central_last(padded[1:-1, 1:-1])
    magnitude = jnp.sqrt(grad_x * grad_x + grad_y * grad_y + grad_z * grad_z)
    inverse = -1.0 / jnp.maximum(magnitude, grad_floor)
    flow_x = grad_x * inverse
    flow_y = grad_y * inverse
    flow_z = (grad_z * inverse)[1:-1, 1:-1]
    return (
        0.5 * (flow_x[2:, 1:-1] - flow_x[:-2, 1:-1])
        + 0.5 * (flow_y[1:-1, 2:] - flow_y[1:-1, :-2])
        + central_last(flow_z)
    )


def per_device(sources, labels):
    length = sources.shape[2]
    heat_time = (length / 8.0) ** 2
    grad_floor = 0.04 / heat_time
    wide = lax.axis_size("wide")
    layers = length // wide
    place = lax.axis_index("wide")
    green, moments = column_tables(length, lax.axis_size("narrow"))
    tables = (jnp.asarray(cas_table(length)), jnp.asarray(green), jnp.asarray(moments))

    def mine(table):
        return lax.dynamic_slice_in_dim(jnp.asarray(table), place * layers, layers, axis=0)

    heat_decay = mine(decay_table(length, 1.0 / heat_time))
    line_decay = mine(decay_table(length, 0.0))
    corner = (jnp.arange(length, dtype=jnp.int32)[None, :] == 0) & (place == 0)
    norm = float(length) ** 2
    heat_field = solve(
        sources, tables, heat_decay, heat_decay * (1.0 / (heat_time * norm)),
        jnp.zeros((1, length), jnp.float32),
    )
    divergence = flow_divergence(heat_field, grad_floor)
    return solve(
        divergence, tables, line_decay, line_decay * (-1.0 / norm), jnp.where(corner, -1.0 / norm, 0.0), labels
    )


def solution(mesh):
    return jax.shard_map(
        per_device,
        mesh=mesh,
        in_specs=(P("wide", "narrow", None), P("wide", "narrow", None)),
        out_specs=P("wide", "narrow", None),
        check_vma=False,
    )
```

```python
from functools import partial
import math

import jax
import jax.numpy as jnp
from jax import lax
from jax.experimental import pallas as pl
from jax.experimental.pallas import tpu as pltpu
from jax.sharding import PartitionSpec as P
import numpy as np

highest = lax.Precision.HIGHEST
moment_rows = 8
lanes = 128


def cas_table(length):
    positions = np.arange(length)
    angles = (positions[:, None] * positions[None, :] % length) * (2.0 * math.pi / length)
    return (np.cos(angles) + np.sin(angles)).astype(np.float32)


def decay_table(length, shift):
    eigen = 4.0 * np.sin(np.pi * np.arange(length) / length) ** 2
    lam = shift + eigen[:, None] + eigen[None, :]
    return np.where(lam > 0.0, np.exp(-2.0 * np.arcsinh(0.5 * np.sqrt(lam))), 0.0).astype(np.float32)


def column_tables(length, blocks):
    span = length // blocks
    const = (length * length - 1.0) / (12.0 * length)
    j = np.arange(span, dtype=np.float64)
    gap = np.abs(j[:, None] - j[None, :])
    parts = [gap * (gap - length) / (2.0 * length) + const]
    centred = j - (span - 1) / 2.0
    for delta in range(1, blocks):
        a = centred + length - span * delta
        rows = np.zeros((span, moment_rows))
        rows[:, 0] = (a * a - length * a) / (2.0 * length) + const
        rows[:, 1] = -(2.0 * a - length) / (2.0 * length)
        rows[:, 2] = 1.0 / (2.0 * length)
        parts.append(rows)
    moments = np.zeros((moment_rows, span))
    moments[0], moments[1], moments[2] = 1.0, centred, centred * centred
    return np.concatenate(parts, axis=1).astype(np.float32), moments.astype(np.float32)


def power(base, exponent):
    result = None
    while exponent:
        if exponent & 1:
            result = base if result is None else result * base
        base = base * base
        exponent >>= 1
    return result


def solve_kernel(n, signed, field, table, decay, scale, green, moments, mask, *rest):
    labels = rest[0] if signed else None
    out, waves, work, outgoing, incoming, sent, arrived, send_sem, recv_sem, wide_send, wide_recv = rest[1:] if signed else rest
    xs, span, length = field.shape
    wide = incoming.shape[1]
    layers = length // wide
    group = lanes // layers
    halves = length // lanes
    chunks = span // group
    parts = wide_send.shape[1]
    each = chunks // parts
    rows_each = span // parts
    step_rows = max(1, 256 // span)
    me = lax.axis_index("narrow")
    here = lax.axis_index("wide")
    mesh_ids = pl.DeviceIdType.MESH
    barrier = pltpu.get_barrier_semaphore()
    for step in range(1, n):
        pl.semaphore_signal(barrier, inc=1, device_id={"narrow": lax.rem(me + step, n)}, device_id_type=mesh_ids)

    def greet(step, carry):
        pl.semaphore_signal(barrier, inc=1, device_id={"wide": lax.rem(here + step, wide)}, device_id_type=mesh_ids)
        return carry

    lax.fori_loop(1, wide, greet, 0)

    def block_copy(turn, part, step):
        target = lax.rem(here + step, wide)
        some = pl.ds(part * each, each)
        return pltpu.make_async_remote_copy(
            src_ref=outgoing.at[turn, target, some],
            dst_ref=incoming.at[turn, here, some],
            send_sem=wide_send.at[turn, part, step],
            recv_sem=wide_recv.at[turn, part, step],
            device_id={"wide": target},
            device_id_type=mesh_ids,
        )

    def send_part(turn, part):
        def one(step, carry):
            block_copy(turn, part, step).start()
            return carry

        lax.fori_loop(1, wide, one, 0)
        some = pl.ds(part * each, each)
        incoming[turn, here, some] = outgoing[turn, here, some]

    def receive_part(turn, part):
        def one(step, carry):
            block_copy(turn, part, step).wait_recv()
            return carry

        lax.fori_loop(1, wide, one, 0)

    def finish_part(turn, part):
        def one(step, carry):
            block_copy(turn, part, step).wait_send()
            return carry

        lax.fori_loop(1, wide, one, 0)

    def transform(c, carry):
        rows = field[pl.ds(c * step_rows, step_rows)].astype(jnp.float32).reshape(step_rows * span, length)
        result = jnp.dot(rows, table[...], precision=highest, preferred_element_type=jnp.float32)
        start = pl.multiple_of(c * step_rows * span, step_rows * span)
        for h in range(halves):
            waves[h, pl.ds(start, step_rows * span), :] = result[:, h * lanes : (h + 1) * lanes]
        return carry

    lax.fori_loop(0, xs // step_rows, transform, 0)
    slot_of = lax.broadcasted_iota(jnp.int32, (xs, lanes), 1) // layers

    def split(g, carry):
        for h in range(halves):
            pieces = [waves[h, pl.ds(g * group + i, xs, stride=span), :] for i in range(group)]
            for slot in range(group):
                total = None
                for i in range(group):
                    shift = ((i - slot) * layers) % lanes
                    moved = pltpu.roll(pieces[i], shift, 1) if shift else pieces[i]
                    total = moved if total is None else jnp.where(slot_of == i, moved, total)
                outgoing[0, h * group + slot, g] = total
        return carry

    for part in range(parts):
        lax.fori_loop(part * each, (part + 1) * each, split, 0)
        if part == 0:
            pl.semaphore_wait(barrier, n - 1 + wide - 1)
        send_part(0, part)

    r = decay[...]
    s = scale[...]

    def to_waves(c, carry):
        block = lax.dot_general(
            incoming[0, :, c].reshape(length, lanes).T, table[...], (((1,), (0,)), ((), ())), precision=highest,
            preferred_element_type=jnp.float32,
        )
        work[pl.ds(c * group, group)] = block.reshape(group, layers, length)
        return carry

    for part in range(parts):
        receive_part(0, part)
        lax.fori_loop(part * each, (part + 1) * each, to_waves, 0)

    column = work[:, 0, :]
    sent[2 * layers :, :] = jnp.dot(moments[...], column, precision=highest, preferred_element_type=jnp.float32)

    def ahead(j, v):
        v = work[j] + r * v
        work[j] = v
        return v

    v_last = lax.fori_loop(0, span, ahead, jnp.zeros_like(r), unroll=4)

    def back(i, u):
        j = span - 1 - i
        u = s * work[j] + r * u
        work[j] = u
        return u

    u_first = lax.fori_loop(0, span, back, jnp.zeros_like(r), unroll=4)
    sent[0:layers, :] = v_last
    sent[layers : 2 * layers, :] = u_first
    copies = []
    for step in range(1, n):
        copy = pltpu.make_async_remote_copy(
            src_ref=sent,
            dst_ref=arrived.at[n - 1 - step],
            send_sem=send_sem.at[step - 1],
            recv_sem=recv_sem.at[n - 1 - step],
            device_id={"narrow": lax.rem(me + step, n)},
            device_id_type=mesh_ids,
        )
        copy.start()
        copies.append(copy)
    for part in range(parts):
        finish_part(0, part)
    q = power(r, span)
    close = 1.0 / (1.0 - power(q, n))
    factor = s / (1.0 - r * r)
    tail = q * r
    edge = r - tail * q
    for copy in copies:
        copy.wait()
    stacked = jnp.concatenate([column] + [arrived[d, 2 * layers :, :] for d in range(n - 1)], axis=0)
    extra = jnp.dot(green[...], stacked, precision=highest, preferred_element_type=jnp.float32) * mask[...]
    last = [v_last] + [arrived[d, 0:layers, :] for d in range(n - 1)]
    first = [u_first] + [arrived[d, layers : 2 * layers, :] for d in range(n - 1)]
    alphas = []
    for t in range(n):
        total = last[t % n]
        for k in range(n - 2, -1, -1):
            total = last[(t - 1 - k) % n] + q * total
        alphas.append(total * close * factor)
    begin = [first[t] + alphas[t] * edge for t in range(n)]
    total = begin[0]
    for k in range(n - 2, -1, -1):
        total = begin[(1 + k) % n] + q * total
    inflow = total * close

    def add_ahead(j, p):
        work[j] = work[j] + p
        return p * r

    lax.fori_loop(0, span, add_ahead, alphas[0] * r, unroll=4)
    work[:, 0, :] = work[:, 0, :] + extra

    def add_back(i, p):
        j = span - 1 - i
        work[j] = work[j] + p
        return p * r

    def from_waves(c, carry):
        block = work[pl.ds(c * group, group)].reshape(lanes, length)
        result = lax.dot_general(
            table[...], block, (((1,), (1,)), ((), ())), precision=highest, preferred_element_type=jnp.float32
        )
        outgoing[1, :, c] = result.reshape(wide, xs, lanes)
        return carry

    p = (inflow - alphas[0] * tail) * r
    for turn in range(parts):
        part = parts - 1 - turn
        p = lax.fori_loop(turn * rows_each, (turn + 1) * rows_each, add_back, p, unroll=4)
        lax.fori_loop(part * each, (part + 1) * each, from_waves, 0)
        send_part(1, part)

    def join(g, carry):
        for h in range(halves):
            pieces = [incoming[1, h * group + slot, g] for slot in range(group)]
            for i in range(group):
                total = None
                for slot in range(group):
                    shift = ((slot - i) * layers) % lanes
                    moved = pltpu.roll(pieces[slot], shift, 1) if shift else pieces[slot]
                    total = moved if total is None else jnp.where(slot_of == slot, moved, total)
                waves[h, pl.ds(g * group + i, xs, stride=span), :] = total
        return carry

    for part in reversed(range(parts)):
        receive_part(1, part)
        lax.fori_loop(part * each, (part + 1) * each, join, 0)

    def transform_back(c, carry):
        start = pl.multiple_of(c * step_rows * span, step_rows * span)
        rows = jnp.concatenate([waves[h, pl.ds(start, step_rows * span), :] for h in range(halves)], axis=1)
        result = jnp.dot(rows, table[...], precision=highest, preferred_element_type=jnp.float32)
        result = result.reshape(step_rows, span, length)
        if signed:
            result = result * (2 * labels[pl.ds(c * step_rows, step_rows)] - 1).astype(jnp.float32)
        out[pl.ds(c * step_rows, step_rows)] = result
        return carry

    lax.fori_loop(0, xs // step_rows, transform_back, 0)
    for part in range(parts):
        finish_part(1, part)


def solve(real_field, tables, decay, scale, mask, labels=None):
    xs, span, length = real_field.shape
    n = lax.axis_size("narrow")
    wide = lax.axis_size("wide")
    layers = length // wide
    chunks = span * layers // lanes
    parts = min(4, chunks)
    rows = 2 * layers + moment_rows
    vmem = pl.BlockSpec(memory_space=pltpu.VMEM)
    args = (real_field, tables[0], decay, scale, tables[1], tables[2], mask) + (() if labels is None else (labels,))
    return pl.pallas_call(
        partial(solve_kernel, n, labels is not None),
        out_shape=jax.ShapeDtypeStruct(real_field.shape, jnp.float32),
        in_specs=[vmem] * len(args),
        out_specs=vmem,
        scratch_shapes=[
            pltpu.VMEM((length // lanes, xs * span, lanes), jnp.float32),
            pltpu.VMEM((span, layers, length), jnp.float32),
            pltpu.VMEM((2, wide, chunks, xs, lanes), jnp.float32),
            pltpu.VMEM((2, wide, chunks, xs, lanes), jnp.float32),
            pltpu.VMEM((rows, length), jnp.float32),
            pltpu.VMEM((n - 1, rows, length), jnp.float32),
            pltpu.SemaphoreType.DMA((n - 1,)),
            pltpu.SemaphoreType.DMA((n - 1,)),
            pltpu.SemaphoreType.DMA((2, parts, wide)),
            pltpu.SemaphoreType.DMA((2, parts, wide)),
        ],
        compiler_params=pltpu.CompilerParams(
            collective_id=0 if labels is None else 1, has_side_effects=True, vmem_limit_bytes=40 * 1024 * 1024
        ),
        cost_estimate=pl.CostEstimate(
            flops=8 * xs * span * length * length, bytes_accessed=8 * xs * span * length, transcendentals=0
        ),
        name="solve" if labels is None else "solve_signed",
    )(*args)


def extended(x, sides, width):
    for axis, dim in sides:
        peers, length = (lax.axis_size(axis), x.shape[dim])
        up = [(i, (i + 1) % peers) for i in range(peers)]
        down = [(j, i) for i, j in up]
        last = lax.slice_in_dim(x, length - width, length, axis=dim)
        initial = lax.slice_in_dim(x, 0, width, axis=dim)
        before = lax.ppermute(last, axis, up)
        after = lax.ppermute(initial, axis, down)
        x = jnp.concatenate([before, x, after], axis=dim)
    return x


def central_last(values):
    return 0.5 * (jnp.roll(values, -1, values.ndim - 1) - jnp.roll(values, 1, values.ndim - 1))


def flow_divergence(heat_field, grad_floor):
    padded = extended(heat_field, (("wide", 0), ("narrow", 1)), 2)
    grad_x = 0.5 * (padded[2:, 1:-1] - padded[:-2, 1:-1])
    grad_y = 0.5 * (padded[1:-1, 2:] - padded[1:-1, :-2])
    grad_z = central_last(padded[1:-1, 1:-1])
    magnitude = jnp.sqrt(grad_x * grad_x + grad_y * grad_y + grad_z * grad_z)
    inverse = -1.0 / jnp.maximum(magnitude, grad_floor)
    flow_x = grad_x * inverse
    flow_y = grad_y * inverse
    flow_z = (grad_z * inverse)[1:-1, 1:-1]
    return (
        0.5 * (flow_x[2:, 1:-1] - flow_x[:-2, 1:-1])
        + 0.5 * (flow_y[1:-1, 2:] - flow_y[1:-1, :-2])
        + central_last(flow_z)
    )


def per_device(sources, labels):
    length = sources.shape[2]
    heat_time = (length / 8.0) ** 2
    grad_floor = 0.04 / heat_time
    wide = lax.axis_size("wide")
    layers = length // wide
    place = lax.axis_index("wide")
    green, moments = column_tables(length, lax.axis_size("narrow"))
    tables = (jnp.asarray(cas_table(length)), jnp.asarray(green), jnp.asarray(moments))

    def mine(table):
        return lax.dynamic_slice_in_dim(jnp.asarray(table), place * layers, layers, axis=0)

    heat_decay = mine(decay_table(length, 1.0 / heat_time))
    line_decay = mine(decay_table(length, 0.0))
    corner = (jnp.arange(length, dtype=jnp.int32)[None, :] == 0) & (place == 0)
    norm = float(length) ** 2
    heat_field = solve(
        sources, tables, heat_decay, heat_decay * (1.0 / (heat_time * norm)),
        jnp.zeros((1, length), jnp.float32),
    )
    divergence = flow_divergence(heat_field, grad_floor)
    return solve(
        divergence, tables, line_decay, line_decay * (-1.0 / norm), jnp.where(corner, -1.0 / norm, 0.0), labels
    )


def solution(mesh):
    return jax.shard_map(
        per_device,
        mesh=mesh,
        in_specs=(P("wide", "narrow", None), P("wide", "narrow", None)),
        out_specs=P("wide", "narrow", None),
        check_vma=False,
    )
```

```python
from functools import partial
import math

import jax
import jax.numpy as jnp
from jax import lax
from jax.experimental import pallas as pl
from jax.experimental.pallas import tpu as pltpu
from jax.sharding import PartitionSpec as P
import numpy as np

highest = lax.Precision.HIGHEST
moment_rows = 8
lanes = 128
margin = 8


def cas_table(length):
    positions = np.arange(length)
    angles = (positions[:, None] * positions[None, :] % length) * (2.0 * math.pi / length)
    return (np.cos(angles) + np.sin(angles)).astype(np.float32)


def decay_table(length, shift):
    eigen = 4.0 * np.sin(np.pi * np.arange(length) / length) ** 2
    lam = shift + eigen[:, None] + eigen[None, :]
    return np.where(lam > 0.0, np.exp(-2.0 * np.arcsinh(0.5 * np.sqrt(lam))), 0.0).astype(np.float32)


def column_tables(length, blocks):
    span = length // blocks
    const = (length * length - 1.0) / (12.0 * length)
    j = np.arange(span, dtype=np.float64)
    gap = np.abs(j[:, None] - j[None, :])
    parts = [gap * (gap - length) / (2.0 * length) + const]
    centred = j - (span - 1) / 2.0
    for delta in range(1, blocks):
        a = centred + length - span * delta
        rows = np.zeros((span, moment_rows))
        rows[:, 0] = (a * a - length * a) / (2.0 * length) + const
        rows[:, 1] = -(2.0 * a - length) / (2.0 * length)
        rows[:, 2] = 1.0 / (2.0 * length)
        parts.append(rows)
    moments = np.zeros((moment_rows, span))
    moments[0], moments[1], moments[2] = 1.0, centred, centred * centred
    return np.concatenate(parts, axis=1).astype(np.float32), moments.astype(np.float32)


def power(base, exponent):
    result = None
    while exponent:
        if exponent & 1:
            result = base if result is None else result * base
        base = base * base
        exponent >>= 1
    return result


def flow_stage(n, grad_floor, field, partial_sum, flow_x, padded, leaving, landing, send_sem, recv_sem):
    xs, span, length = field.shape
    me = lax.axis_index("narrow")
    here = lax.axis_index("wide")
    wide = lax.axis_size("wide")
    inside = pl.ds(margin, span)

    def transfer(k, src, dst, target):
        copy = pltpu.make_async_remote_copy(
            src_ref=src, dst_ref=dst, send_sem=send_sem.at[k], recv_sem=recv_sem.at[k],
            device_id=target, device_id_type=pl.DeviceIdType.MESH,
        )
        copy.start()
        return copy

    first = transfer(0, field.at[pl.ds(xs - 2, 2)], padded.at[pl.ds(0, 2), inside], {"wide": lax.rem(here + 1, wide)})
    second = transfer(1, field.at[pl.ds(0, 2)], padded.at[pl.ds(xs + 2, 2), inside], {"wide": lax.rem(here + wide - 1, wide)})
    edge = jnp.zeros((xs + 4, margin, length), jnp.float32)
    padded[:, 0:margin, :] = edge
    padded[:, margin + span :, :] = edge

    def fill(x, carry):
        padded[x + 2, margin : margin + span, :] = field[x]
        return carry

    lax.fori_loop(0, xs, fill, 0)
    first.wait()
    second.wait()
    for row in range(2):
        leaving[0, row] = padded[:, margin + span - 2 + row, :]
        leaving[1, row] = padded[:, margin + row, :]
    third = transfer(2, leaving.at[0], landing.at[0], {"narrow": lax.rem(me + 1, n)})
    fourth = transfer(3, leaving.at[1], landing.at[1], {"narrow": lax.rem(me + n - 1, n)})
    third.wait()
    fourth.wait()
    for row in range(2):
        padded[:, margin - 2 + row, :] = landing[0, row]
        padded[:, margin + span + row, :] = landing[1, row]

    def central(values, dim):
        size = values.shape[dim]
        return 0.5 * (pltpu.roll(values, size - 1, dim) - pltpu.roll(values, 1, dim))

    def plane(p, carry):
        values = padded[p]
        grad_x = 0.5 * (padded[p + 1] - padded[p - 1])
        grad_y = central(values, 0)
        grad_z = central(values, 1)
        magnitude = jnp.sqrt(grad_x * grad_x + grad_y * grad_y + grad_z * grad_z)
        inverse = -1.0 / jnp.maximum(magnitude, grad_floor)
        flow_x[p - 1] = (grad_x * inverse)[margin : margin + span]
        total = central(grad_y * inverse, 0) + central(grad_z * inverse, 1)
        partial_sum[p - 1] = total[margin : margin + span]
        return carry

    lax.fori_loop(1, xs + 3, plane, 0)


def solve_kernel(n, grad_floor, field, table, decay, scale, green, moments, mask, *rest):
    signed = grad_floor is not None
    labels = rest[0] if signed else None
    rest = rest[1:] if signed else rest
    out, waves, work, outgoing, incoming, sent, arrived, send_sem, recv_sem, wide_send, wide_recv = rest[:11]
    xs, span, length = field.shape
    wide = incoming.shape[1]
    layers = length // wide
    group = lanes // layers
    halves = length // lanes
    chunks = span // group
    parts = wide_send.shape[1]
    each = chunks // parts
    rows_each = span // parts
    step_rows = max(1, 256 // span)
    me = lax.axis_index("narrow")
    here = lax.axis_index("wide")
    mesh_ids = pl.DeviceIdType.MESH
    barrier = pltpu.get_barrier_semaphore()
    for step in range(1, n):
        pl.semaphore_signal(barrier, inc=1, device_id={"narrow": lax.rem(me + step, n)}, device_id_type=mesh_ids)

    def greet(step, carry):
        pl.semaphore_signal(barrier, inc=1, device_id={"wide": lax.rem(here + step, wide)}, device_id_type=mesh_ids)
        return carry

    lax.fori_loop(1, wide, greet, 0)

    if signed:
        pl.semaphore_wait(barrier, n - 1 + wide - 1)
        partial_sum, flow_x = rest[11:13]
        flow_stage(n, grad_floor, field, *rest[11:])

    def block_copy(turn, part, step):
        target = lax.rem(here + step, wide)
        some = pl.ds(part * each, each)
        return pltpu.make_async_remote_copy(
            src_ref=outgoing.at[turn, target, some],
            dst_ref=incoming.at[turn, here, some],
            send_sem=wide_send.at[turn, part, step],
            recv_sem=wide_recv.at[turn, part, step],
            device_id={"wide": target},
            device_id_type=mesh_ids,
        )

    def send_part(turn, part):
        def one(step, carry):
            block_copy(turn, part, step).start()
            return carry

        lax.fori_loop(1, wide, one, 0)
        some = pl.ds(part * each, each)
        incoming[turn, here, some] = outgoing[turn, here, some]

    def receive_part(turn, part):
        def one(step, carry):
            block_copy(turn, part, step).wait_recv()
            return carry

        lax.fori_loop(1, wide, one, 0)

    def finish_part(turn, part):
        def one(step, carry):
            block_copy(turn, part, step).wait_send()
            return carry

        lax.fori_loop(1, wide, one, 0)

    def transform(c, carry):
        if signed:
            planes = partial_sum[pl.ds(1 + c * step_rows, step_rows)] + 0.5 * (
                flow_x[pl.ds(2 + c * step_rows, step_rows)] - flow_x[pl.ds(c * step_rows, step_rows)]
            )
        else:
            planes = field[pl.ds(c * step_rows, step_rows)].astype(jnp.float32)
        rows = planes.reshape(step_rows * span, length)
        result = jnp.dot(rows, table[...], precision=highest, preferred_element_type=jnp.float32)
        start = pl.multiple_of(c * step_rows * span, step_rows * span)
        for h in range(halves):
            waves[h, pl.ds(start, step_rows * span), :] = result[:, h * lanes : (h + 1) * lanes]
        return carry

    lax.fori_loop(0, xs // step_rows, transform, 0)
    slot_of = lax.broadcasted_iota(jnp.int32, (xs, lanes), 1) // layers

    def split(g, carry):
        for h in range(halves):
            pieces = [waves[h, pl.ds(g * group + i, xs, stride=span), :] for i in range(group)]
            for slot in range(group):
                total = None
                for i in range(group):
                    shift = ((i - slot) * layers) % lanes
                    moved = pltpu.roll(pieces[i], shift, 1) if shift else pieces[i]
                    total = moved if total is None else jnp.where(slot_of == i, moved, total)
                outgoing[0, h * group + slot, g] = total
        return carry

    for part in range(parts):
        lax.fori_loop(part * each, (part + 1) * each, split, 0)
        if part == 0 and not signed:
            pl.semaphore_wait(barrier, n - 1 + wide - 1)
        send_part(0, part)

    r = decay[...]
    s = scale[...]

    def to_waves(c, carry):
        block = lax.dot_general(
            incoming[0, :, c].reshape(length, lanes).T, table[...], (((1,), (0,)), ((), ())), precision=highest,
            preferred_element_type=jnp.float32,
        )
        work[pl.ds(c * group, group)] = block.reshape(group, layers, length)
        return carry

    for part in range(parts):
        receive_part(0, part)
        lax.fori_loop(part * each, (part + 1) * each, to_waves, 0)

    column = work[:, 0, :]
    sent[2 * layers :, :] = jnp.dot(moments[...], column, precision=highest, preferred_element_type=jnp.float32)

    def ahead(j, v):
        v = work[j] + r * v
        work[j] = v
        return v

    v_last = lax.fori_loop(0, span, ahead, jnp.zeros_like(r), unroll=4)

    def back(i, u):
        j = span - 1 - i
        u = s * work[j] + r * u
        work[j] = u
        return u

    u_first = lax.fori_loop(0, span, back, jnp.zeros_like(r), unroll=4)
    sent[0:layers, :] = v_last
    sent[layers : 2 * layers, :] = u_first
    copies = []
    for step in range(1, n):
        copy = pltpu.make_async_remote_copy(
            src_ref=sent,
            dst_ref=arrived.at[n - 1 - step],
            send_sem=send_sem.at[step - 1],
            recv_sem=recv_sem.at[n - 1 - step],
            device_id={"narrow": lax.rem(me + step, n)},
            device_id_type=mesh_ids,
        )
        copy.start()
        copies.append(copy)
    for part in range(parts):
        finish_part(0, part)
    q = power(r, span)
    close = 1.0 / (1.0 - power(q, n))
    factor = s / (1.0 - r * r)
    tail = q * r
    edge = r - tail * q
    for copy in copies:
        copy.wait()
    stacked = jnp.concatenate([column] + [arrived[d, 2 * layers :, :] for d in range(n - 1)], axis=0)
    extra = jnp.dot(green[...], stacked, precision=highest, preferred_element_type=jnp.float32) * mask[...]
    last = [v_last] + [arrived[d, 0:layers, :] for d in range(n - 1)]
    first = [u_first] + [arrived[d, layers : 2 * layers, :] for d in range(n - 1)]
    alphas = []
    for t in range(n):
        total = last[t % n]
        for k in range(n - 2, -1, -1):
            total = last[(t - 1 - k) % n] + q * total
        alphas.append(total * close * factor)
    begin = [first[t] + alphas[t] * edge for t in range(n)]
    total = begin[0]
    for k in range(n - 2, -1, -1):
        total = begin[(1 + k) % n] + q * total
    inflow = total * close

    def add_ahead(j, p):
        work[j] = work[j] + p
        return p * r

    lax.fori_loop(0, span, add_ahead, alphas[0] * r, unroll=4)
    work[:, 0, :] = work[:, 0, :] + extra

    def add_back(i, p):
        j = span - 1 - i
        work[j] = work[j] + p
        return p * r

    def from_waves(c, carry):
        block = work[pl.ds(c * group, group)].reshape(lanes, length)
        result = lax.dot_general(
            table[...], block, (((1,), (1,)), ((), ())), precision=highest, preferred_element_type=jnp.float32
        )
        outgoing[1, :, c] = result.reshape(wide, xs, lanes)
        return carry

    p = (inflow - alphas[0] * tail) * r
    for turn in range(parts):
        part = parts - 1 - turn
        p = lax.fori_loop(turn * rows_each, (turn + 1) * rows_each, add_back, p, unroll=4)
        lax.fori_loop(part * each, (part + 1) * each, from_waves, 0)
        send_part(1, part)

    def join(g, carry):
        for h in range(halves):
            pieces = [incoming[1, h * group + slot, g] for slot in range(group)]
            for i in range(group):
                total = None
                for slot in range(group):
                    shift = ((slot - i) * layers) % lanes
                    moved = pltpu.roll(pieces[slot], shift, 1) if shift else pieces[slot]
                    total = moved if total is None else jnp.where(slot_of == slot, moved, total)
                waves[h, pl.ds(g * group + i, xs, stride=span), :] = total
        return carry

    for part in reversed(range(parts)):
        receive_part(1, part)
        lax.fori_loop(part * each, (part + 1) * each, join, 0)

    def transform_back(c, carry):
        start = pl.multiple_of(c * step_rows * span, step_rows * span)
        rows = jnp.concatenate([waves[h, pl.ds(start, step_rows * span), :] for h in range(halves)], axis=1)
        result = jnp.dot(rows, table[...], precision=highest, preferred_element_type=jnp.float32)
        result = result.reshape(step_rows, span, length)
        if signed:
            result = result * (2 * labels[pl.ds(c * step_rows, step_rows)] - 1).astype(jnp.float32)
        out[pl.ds(c * step_rows, step_rows)] = result
        return carry

    lax.fori_loop(0, xs // step_rows, transform_back, 0)
    for part in range(parts):
        finish_part(1, part)


def solve(real_field, tables, decay, scale, mask, labels=None, grad_floor=None):
    xs, span, length = real_field.shape
    n = lax.axis_size("narrow")
    wide = lax.axis_size("wide")
    layers = length // wide
    chunks = span * layers // lanes
    parts = min(4, chunks)
    rows = 2 * layers + moment_rows
    vmem = pl.BlockSpec(memory_space=pltpu.VMEM)
    args = (real_field, tables[0], decay, scale, tables[1], tables[2], mask) + (() if labels is None else (labels,))
    flow_scratch = [] if labels is None else [
        pltpu.VMEM((xs + 2, span, length), jnp.float32),
        pltpu.VMEM((xs + 2, span, length), jnp.float32),
        pltpu.VMEM((xs + 4, span + 2 * margin, length), jnp.float32),
        pltpu.VMEM((2, 2, xs + 4, length), jnp.float32),
        pltpu.VMEM((2, 2, xs + 4, length), jnp.float32),
        pltpu.SemaphoreType.DMA((4,)),
        pltpu.SemaphoreType.DMA((4,)),
    ]
    return pl.pallas_call(
        partial(solve_kernel, n, grad_floor),
        out_shape=jax.ShapeDtypeStruct(real_field.shape, jnp.float32),
        in_specs=[vmem] * len(args),
        out_specs=vmem,
        scratch_shapes=[
            pltpu.VMEM((length // lanes, xs * span, lanes), jnp.float32),
            pltpu.VMEM((span, layers, length), jnp.float32),
            pltpu.VMEM((2, wide, chunks, xs, lanes), jnp.float32),
            pltpu.VMEM((2, wide, chunks, xs, lanes), jnp.float32),
            pltpu.VMEM((rows, length), jnp.float32),
            pltpu.VMEM((n - 1, rows, length), jnp.float32),
            pltpu.SemaphoreType.DMA((n - 1,)),
            pltpu.SemaphoreType.DMA((n - 1,)),
            pltpu.SemaphoreType.DMA((2, parts, wide)),
            pltpu.SemaphoreType.DMA((2, parts, wide)),
        ]
        + flow_scratch,
        compiler_params=pltpu.CompilerParams(
            collective_id=0 if labels is None else 1, has_side_effects=True, vmem_limit_bytes=40 * 1024 * 1024
        ),
        cost_estimate=pl.CostEstimate(
            flops=8 * xs * span * length * length, bytes_accessed=8 * xs * span * length, transcendentals=0
        ),
        name="solve" if labels is None else "solve_signed",
    )(*args)


def per_device(sources, labels):
    length = sources.shape[2]
    heat_time = (length / 8.0) ** 2
    grad_floor = 0.04 / heat_time
    wide = lax.axis_size("wide")
    layers = length // wide
    place = lax.axis_index("wide")
    green, moments = column_tables(length, lax.axis_size("narrow"))
    tables = (jnp.asarray(cas_table(length)), jnp.asarray(green), jnp.asarray(moments))

    def mine(table):
        return lax.dynamic_slice_in_dim(jnp.asarray(table), place * layers, layers, axis=0)

    heat_decay = mine(decay_table(length, 1.0 / heat_time))
    line_decay = mine(decay_table(length, 0.0))
    corner = (jnp.arange(length, dtype=jnp.int32)[None, :] == 0) & (place == 0)
    norm = float(length) ** 2
    heat_field = solve(
        sources, tables, heat_decay, heat_decay * (1.0 / (heat_time * norm)),
        jnp.zeros((1, length), jnp.float32),
    )
    return solve(
        heat_field, tables, line_decay, line_decay * (-1.0 / norm), jnp.where(corner, -1.0 / norm, 0.0), labels,
        grad_floor,
    )


def solution(mesh):
    return jax.shard_map(
        per_device,
        mesh=mesh,
        in_specs=(P("wide", "narrow", None), P("wide", "narrow", None)),
        out_specs=P("wide", "narrow", None),
        check_vma=False,
    )
```

```python
from functools import partial
import math

import jax
import jax.numpy as jnp
from jax import lax
from jax.experimental import pallas as pl
from jax.experimental.pallas import tpu as pltpu
from jax.sharding import PartitionSpec as P
import numpy as np

highest = lax.Precision.HIGHEST
moment_rows = 8
lanes = 128
margin = 8


def cas_table(length):
    positions = np.arange(length)
    angles = (positions[:, None] * positions[None, :] % length) * (2.0 * math.pi / length)
    return (np.cos(angles) + np.sin(angles)).astype(np.float32)


def decay_table(length, shift):
    eigen = 4.0 * np.sin(np.pi * np.arange(length) / length) ** 2
    lam = shift + eigen[:, None] + eigen[None, :]
    return np.where(lam > 0.0, np.exp(-2.0 * np.arcsinh(0.5 * np.sqrt(lam))), 0.0).astype(np.float32)


def column_tables(length, blocks):
    span = length // blocks
    const = (length * length - 1.0) / (12.0 * length)
    j = np.arange(span, dtype=np.float64)
    gap = np.abs(j[:, None] - j[None, :])
    parts = [gap * (gap - length) / (2.0 * length) + const]
    centred = j - (span - 1) / 2.0
    for delta in range(1, blocks):
        a = centred + length - span * delta
        rows = np.zeros((span, moment_rows))
        rows[:, 0] = (a * a - length * a) / (2.0 * length) + const
        rows[:, 1] = -(2.0 * a - length) / (2.0 * length)
        rows[:, 2] = 1.0 / (2.0 * length)
        parts.append(rows)
    moments = np.zeros((moment_rows, span))
    moments[0], moments[1], moments[2] = 1.0, centred, centred * centred
    return np.concatenate(parts, axis=1).astype(np.float32), moments.astype(np.float32)


def power(base, exponent):
    result = None
    while exponent:
        if exponent & 1:
            result = base if result is None else result * base
        base = base * base
        exponent >>= 1
    return result


def flow_stage(n, grad_floor, field, partial_sum, flow_x, padded, leaving, landing, send_sem, recv_sem):
    xs, span, length = field.shape
    me = lax.axis_index("narrow")
    here = lax.axis_index("wide")
    wide = lax.axis_size("wide")
    inside = pl.ds(margin, span)

    def transfer(k, src, dst, target):
        copy = pltpu.make_async_remote_copy(
            src_ref=src, dst_ref=dst, send_sem=send_sem.at[k], recv_sem=recv_sem.at[k],
            device_id=target, device_id_type=pl.DeviceIdType.MESH,
        )
        copy.start()
        return copy

    first = transfer(0, field.at[pl.ds(xs - 2, 2)], padded.at[pl.ds(0, 2), inside], {"wide": lax.rem(here + 1, wide)})
    second = transfer(1, field.at[pl.ds(0, 2)], padded.at[pl.ds(xs + 2, 2), inside], {"wide": lax.rem(here + wide - 1, wide)})
    edge = jnp.zeros((xs + 4, margin, length), jnp.float32)
    padded[:, 0:margin, :] = edge
    padded[:, margin + span :, :] = edge

    def fill(x, carry):
        padded[x + 2, margin : margin + span, :] = field[x]
        return carry

    lax.fori_loop(0, xs, fill, 0)
    first.wait()
    second.wait()
    for row in range(2):
        leaving[0, row] = padded[:, margin + span - 2 + row, :]
        leaving[1, row] = padded[:, margin + row, :]
    third = transfer(2, leaving.at[0], landing.at[0], {"narrow": lax.rem(me + 1, n)})
    fourth = transfer(3, leaving.at[1], landing.at[1], {"narrow": lax.rem(me + n - 1, n)})
    third.wait()
    fourth.wait()
    for row in range(2):
        padded[:, margin - 2 + row, :] = landing[0, row]
        padded[:, margin + span + row, :] = landing[1, row]

    def central(values, dim):
        size = values.shape[dim]
        return 0.5 * (pltpu.roll(values, size - 1, dim) - pltpu.roll(values, 1, dim))

    def plane(p, carry):
        values = padded[p]
        grad_x = 0.5 * (padded[p + 1] - padded[p - 1])
        grad_y = central(values, 0)
        grad_z = central(values, 1)
        magnitude = jnp.sqrt(grad_x * grad_x + grad_y * grad_y + grad_z * grad_z)
        inverse = -1.0 / jnp.maximum(magnitude, grad_floor)
        flow_x[p - 1] = (grad_x * inverse)[margin : margin + span]
        total = central(grad_y * inverse, 0) + central(grad_z * inverse, 1)
        partial_sum[p - 1] = total[margin : margin + span]
        return carry

    lax.fori_loop(1, xs + 3, plane, 0)


def solve_kernel(n, grad_floor, field, table, decay, scale, green, moments, mask, *rest):
    signed = grad_floor is not None
    labels = rest[0] if signed else None
    rest = rest[1:] if signed else rest
    out, waves, work, outgoing, incoming, sent, arrived, send_sem, recv_sem, wide_send, wide_recv = rest[:11]
    xs, span, length = field.shape
    wide = incoming.shape[1]
    layers = length // wide
    group = lanes // layers
    halves = length // lanes
    chunks = span // group
    parts = wide_send.shape[1]
    each = chunks // parts
    rows_each = span // parts
    step_rows = max(1, 256 // span)
    me = lax.axis_index("narrow")
    here = lax.axis_index("wide")
    mesh_ids = pl.DeviceIdType.MESH
    barrier = pltpu.get_barrier_semaphore()
    for step in range(1, n):
        pl.semaphore_signal(barrier, inc=1, device_id={"narrow": lax.rem(me + step, n)}, device_id_type=mesh_ids)

    def greet(step, carry):
        pl.semaphore_signal(barrier, inc=1, device_id={"wide": lax.rem(here + step, wide)}, device_id_type=mesh_ids)
        return carry

    lax.fori_loop(1, wide, greet, 0)

    if signed:
        pl.semaphore_wait(barrier, n - 1 + wide - 1)
        partial_sum, flow_x = rest[11:13]
        flow_stage(n, grad_floor, field, *rest[11:])

    def block_copy(turn, part, step):
        target = lax.rem(here + step, wide)
        some = pl.ds(part * each, each)
        return pltpu.make_async_remote_copy(
            src_ref=outgoing.at[turn, target, some],
            dst_ref=incoming.at[turn, here, some],
            send_sem=wide_send.at[turn, part, step],
            recv_sem=wide_recv.at[turn, part, step],
            device_id={"wide": target},
            device_id_type=mesh_ids,
        )

    def send_part(turn, part):
        def one(step, carry):
            block_copy(turn, part, step).start()
            return carry

        lax.fori_loop(1, wide, one, 0)
        some = pl.ds(part * each, each)
        incoming[turn, here, some] = outgoing[turn, here, some]

    def receive_part(turn, part):
        def one(step, carry):
            block_copy(turn, part, step).wait_recv()
            return carry

        lax.fori_loop(1, wide, one, 0)

    def finish_part(turn, part):
        def one(step, carry):
            block_copy(turn, part, step).wait_send()
            return carry

        lax.fori_loop(1, wide, one, 0)

    def transform(c, carry):
        if signed:
            planes = partial_sum[pl.ds(1 + c * step_rows, step_rows)] + 0.5 * (
                flow_x[pl.ds(2 + c * step_rows, step_rows)] - flow_x[pl.ds(c * step_rows, step_rows)]
            )
        else:
            planes = field[pl.ds(c * step_rows, step_rows)].astype(jnp.float32)
        rows = planes.reshape(step_rows * span, length)
        result = jnp.dot(rows, table[...], precision=highest, preferred_element_type=jnp.float32)
        start = pl.multiple_of(c * step_rows * span, step_rows * span)
        for h in range(halves):
            waves[h, pl.ds(start, step_rows * span), :] = result[:, h * lanes : (h + 1) * lanes]
        return carry

    lax.fori_loop(0, xs // step_rows, transform, 0)
    slot_of = lax.broadcasted_iota(jnp.int32, (xs, lanes), 1) // layers

    def split(g, carry):
        for h in range(halves):
            pieces = [waves[h, pl.ds(g * group + i, xs, stride=span), :] for i in range(group)]
            for slot in range(group):
                total = None
                for i in range(group):
                    shift = ((i - slot) * layers) % lanes
                    moved = pltpu.roll(pieces[i], shift, 1) if shift else pieces[i]
                    total = moved if total is None else jnp.where(slot_of == i, moved, total)
                outgoing[0, h * group + slot, g] = total
        return carry

    for part in range(parts):
        lax.fori_loop(part * each, (part + 1) * each, split, 0)
        if part == 0 and not signed:
            pl.semaphore_wait(barrier, n - 1 + wide - 1)
        send_part(0, part)

    r = decay[...]
    s = scale[...]

    def to_waves(c, carry):
        block = lax.dot_general(
            incoming[0, :, c].reshape(length, lanes).T, table[...], (((1,), (0,)), ((), ())), precision=highest,
            preferred_element_type=jnp.float32,
        )
        work[pl.ds(c * group, group)] = block.reshape(group, layers, length)
        return carry

    def ahead(j, v):
        v = work[j] + r * v
        work[j] = v
        return v

    v_last = jnp.zeros_like(r)
    columns = []
    for part in range(parts):
        receive_part(0, part)
        lax.fori_loop(part * each, (part + 1) * each, to_waves, 0)
        columns.append(work[part * rows_each : (part + 1) * rows_each, 0, :])
        v_last = lax.fori_loop(part * rows_each, (part + 1) * rows_each, ahead, v_last, unroll=4)
    column = jnp.concatenate(columns, axis=0)
    sent[2 * layers :, :] = jnp.dot(moments[...], column, precision=highest, preferred_element_type=jnp.float32)

    def back(i, u):
        j = span - 1 - i
        u = s * work[j] + r * u
        work[j] = u
        return u

    u_first = lax.fori_loop(0, span, back, jnp.zeros_like(r), unroll=4)
    sent[0:layers, :] = v_last
    sent[layers : 2 * layers, :] = u_first
    copies = []
    for step in range(1, n):
        copy = pltpu.make_async_remote_copy(
            src_ref=sent,
            dst_ref=arrived.at[n - 1 - step],
            send_sem=send_sem.at[step - 1],
            recv_sem=recv_sem.at[n - 1 - step],
            device_id={"narrow": lax.rem(me + step, n)},
            device_id_type=mesh_ids,
        )
        copy.start()
        copies.append(copy)
    for part in range(parts):
        finish_part(0, part)
    q = power(r, span)
    close = 1.0 / (1.0 - power(q, n))
    factor = s / (1.0 - r * r)
    tail = q * r
    edge = r - tail * q
    for copy in copies:
        copy.wait()
    stacked = jnp.concatenate([column] + [arrived[d, 2 * layers :, :] for d in range(n - 1)], axis=0)
    extra = jnp.dot(green[...], stacked, precision=highest, preferred_element_type=jnp.float32) * mask[...]
    last = [v_last] + [arrived[d, 0:layers, :] for d in range(n - 1)]
    first = [u_first] + [arrived[d, layers : 2 * layers, :] for d in range(n - 1)]
    alphas = []
    for t in range(n):
        total = last[t % n]
        for k in range(n - 2, -1, -1):
            total = last[(t - 1 - k) % n] + q * total
        alphas.append(total * close * factor)
    begin = [first[t] + alphas[t] * edge for t in range(n)]
    total = begin[0]
    for k in range(n - 2, -1, -1):
        total = begin[(1 + k) % n] + q * total
    inflow = total * close

    def add_ahead(j, p):
        work[j] = work[j] + p
        return p * r

    lax.fori_loop(0, span, add_ahead, alphas[0] * r, unroll=4)
    work[:, 0, :] = work[:, 0, :] + extra

    def add_back(i, p):
        j = span - 1 - i
        work[j] = work[j] + p
        return p * r

    def from_waves(c, carry):
        block = work[pl.ds(c * group, group)].reshape(lanes, length)
        result = lax.dot_general(
            table[...], block, (((1,), (1,)), ((), ())), precision=highest, preferred_element_type=jnp.float32
        )
        outgoing[1, :, c] = result.reshape(wide, xs, lanes)
        return carry

    p = (inflow - alphas[0] * tail) * r
    for turn in range(parts):
        part = parts - 1 - turn
        p = lax.fori_loop(turn * rows_each, (turn + 1) * rows_each, add_back, p, unroll=4)
        lax.fori_loop(part * each, (part + 1) * each, from_waves, 0)
        send_part(1, part)

    def join(g, carry):
        for h in range(halves):
            pieces = [incoming[1, h * group + slot, g] for slot in range(group)]
            for i in range(group):
                total = None
                for slot in range(group):
                    shift = ((slot - i) * layers) % lanes
                    moved = pltpu.roll(pieces[slot], shift, 1) if shift else pieces[slot]
                    total = moved if total is None else jnp.where(slot_of == slot, moved, total)
                waves[h, pl.ds(g * group + i, xs, stride=span), :] = total
        return carry

    for part in reversed(range(parts)):
        receive_part(1, part)
        lax.fori_loop(part * each, (part + 1) * each, join, 0)

    def transform_back(c, carry):
        start = pl.multiple_of(c * step_rows * span, step_rows * span)
        rows = jnp.concatenate([waves[h, pl.ds(start, step_rows * span), :] for h in range(halves)], axis=1)
        result = jnp.dot(rows, table[...], precision=highest, preferred_element_type=jnp.float32)
        result = result.reshape(step_rows, span, length)
        if signed:
            result = result * (2 * labels[pl.ds(c * step_rows, step_rows)] - 1).astype(jnp.float32)
        out[pl.ds(c * step_rows, step_rows)] = result
        return carry

    lax.fori_loop(0, xs // step_rows, transform_back, 0)
    for part in range(parts):
        finish_part(1, part)


def solve(real_field, tables, decay, scale, mask, labels=None, grad_floor=None):
    xs, span, length = real_field.shape
    n = lax.axis_size("narrow")
    wide = lax.axis_size("wide")
    layers = length // wide
    chunks = span * layers // lanes
    parts = min(8, chunks)
    rows = 2 * layers + moment_rows
    vmem = pl.BlockSpec(memory_space=pltpu.VMEM)
    args = (real_field, tables[0], decay, scale, tables[1], tables[2], mask) + (() if labels is None else (labels,))
    flow_scratch = [] if labels is None else [
        pltpu.VMEM((xs + 2, span, length), jnp.float32),
        pltpu.VMEM((xs + 2, span, length), jnp.float32),
        pltpu.VMEM((xs + 4, span + 2 * margin, length), jnp.float32),
        pltpu.VMEM((2, 2, xs + 4, length), jnp.float32),
        pltpu.VMEM((2, 2, xs + 4, length), jnp.float32),
        pltpu.SemaphoreType.DMA((4,)),
        pltpu.SemaphoreType.DMA((4,)),
    ]
    return pl.pallas_call(
        partial(solve_kernel, n, grad_floor),
        out_shape=jax.ShapeDtypeStruct(real_field.shape, jnp.float32),
        in_specs=[vmem] * len(args),
        out_specs=vmem,
        scratch_shapes=[
            pltpu.VMEM((length // lanes, xs * span, lanes), jnp.float32),
            pltpu.VMEM((span, layers, length), jnp.float32),
            pltpu.VMEM((2, wide, chunks, xs, lanes), jnp.float32),
            pltpu.VMEM((2, wide, chunks, xs, lanes), jnp.float32),
            pltpu.VMEM((rows, length), jnp.float32),
            pltpu.VMEM((n - 1, rows, length), jnp.float32),
            pltpu.SemaphoreType.DMA((n - 1,)),
            pltpu.SemaphoreType.DMA((n - 1,)),
            pltpu.SemaphoreType.DMA((2, parts, wide)),
            pltpu.SemaphoreType.DMA((2, parts, wide)),
        ]
        + flow_scratch,
        compiler_params=pltpu.CompilerParams(
            collective_id=0 if labels is None else 1, has_side_effects=True, vmem_limit_bytes=40 * 1024 * 1024
        ),
        cost_estimate=pl.CostEstimate(
            flops=8 * xs * span * length * length, bytes_accessed=8 * xs * span * length, transcendentals=0
        ),
        name="solve" if labels is None else "solve_signed",
    )(*args)


def per_device(sources, labels):
    length = sources.shape[2]
    heat_time = (length / 8.0) ** 2
    grad_floor = 0.04 / heat_time
    wide = lax.axis_size("wide")
    layers = length // wide
    place = lax.axis_index("wide")
    green, moments = column_tables(length, lax.axis_size("narrow"))
    tables = (jnp.asarray(cas_table(length)), jnp.asarray(green), jnp.asarray(moments))

    def mine(table):
        return lax.dynamic_slice_in_dim(jnp.asarray(table), place * layers, layers, axis=0)

    heat_decay = mine(decay_table(length, 1.0 / heat_time))
    line_decay = mine(decay_table(length, 0.0))
    corner = (jnp.arange(length, dtype=jnp.int32)[None, :] == 0) & (place == 0)
    norm = float(length) ** 2
    heat_field = solve(
        sources, tables, heat_decay, heat_decay * (1.0 / (heat_time * norm)),
        jnp.zeros((1, length), jnp.float32),
    )
    return solve(
        heat_field, tables, line_decay, line_decay * (-1.0 / norm), jnp.where(corner, -1.0 / norm, 0.0), labels,
        grad_floor,
    )


def solution(mesh):
    return jax.shard_map(
        per_device,
        mesh=mesh,
        in_specs=(P("wide", "narrow", None), P("wide", "narrow", None)),
        out_specs=P("wide", "narrow", None),
        check_vma=False,
    )
```

```python
from functools import partial
import math

import jax
import jax.numpy as jnp
from jax import lax
from jax.experimental import pallas as pl
from jax.experimental.pallas import tpu as pltpu
from jax.sharding import PartitionSpec as P
import numpy as np

highest = lax.Precision.HIGHEST
moment_rows = 8
lanes = 128
margin = 8


def cas_table(length):
    positions = np.arange(length)
    angles = (positions[:, None] * positions[None, :] % length) * (2.0 * math.pi / length)
    return (np.cos(angles) + np.sin(angles)).astype(np.float32)


def decay_table(length, shift):
    eigen = 4.0 * np.sin(np.pi * np.arange(length) / length) ** 2
    lam = shift + eigen[:, None] + eigen[None, :]
    return np.where(lam > 0.0, np.exp(-2.0 * np.arcsinh(0.5 * np.sqrt(lam))), 0.0).astype(np.float32)


def column_tables(length, blocks):
    span = length // blocks
    const = (length * length - 1.0) / (12.0 * length)
    j = np.arange(span, dtype=np.float64)
    gap = np.abs(j[:, None] - j[None, :])
    parts = [gap * (gap - length) / (2.0 * length) + const]
    centred = j - (span - 1) / 2.0
    for delta in range(1, blocks):
        a = centred + length - span * delta
        rows = np.zeros((span, moment_rows))
        rows[:, 0] = (a * a - length * a) / (2.0 * length) + const
        rows[:, 1] = -(2.0 * a - length) / (2.0 * length)
        rows[:, 2] = 1.0 / (2.0 * length)
        parts.append(rows)
    moments = np.zeros((moment_rows, span))
    moments[0], moments[1], moments[2] = 1.0, centred, centred * centred
    return np.concatenate(parts, axis=1).astype(np.float32), moments.astype(np.float32)


def power(base, exponent):
    result = None
    while exponent:
        if exponent & 1:
            result = base if result is None else result * base
        base = base * base
        exponent >>= 1
    return result


def flow_stage(n, grad_floor, field, partial_sum, flow_x, padded, leaving, landing, send_sem, recv_sem):
    xs, span, length = field.shape
    me = lax.axis_index("narrow")
    here = lax.axis_index("wide")
    wide = lax.axis_size("wide")
    inside = pl.ds(margin, span)

    def transfer(k, src, dst, target):
        copy = pltpu.make_async_remote_copy(
            src_ref=src, dst_ref=dst, send_sem=send_sem.at[k], recv_sem=recv_sem.at[k],
            device_id=target, device_id_type=pl.DeviceIdType.MESH,
        )
        copy.start()
        return copy

    first = transfer(0, field.at[pl.ds(xs - 2, 2)], padded.at[pl.ds(0, 2), inside], {"wide": lax.rem(here + 1, wide)})
    second = transfer(1, field.at[pl.ds(0, 2)], padded.at[pl.ds(xs + 2, 2), inside], {"wide": lax.rem(here + wide - 1, wide)})
    edge = jnp.zeros((xs + 4, margin, length), jnp.float32)
    padded[:, 0:margin, :] = edge
    padded[:, margin + span :, :] = edge

    def fill(x, carry):
        padded[x + 2, margin : margin + span, :] = field[x]
        return carry

    lax.fori_loop(0, xs, fill, 0)
    first.wait()
    second.wait()
    for row in range(2):
        leaving[0, row] = padded[:, margin + span - 2 + row, :]
        leaving[1, row] = padded[:, margin + row, :]
    third = transfer(2, leaving.at[0], landing.at[0], {"narrow": lax.rem(me + 1, n)})
    fourth = transfer(3, leaving.at[1], landing.at[1], {"narrow": lax.rem(me + n - 1, n)})
    third.wait()
    fourth.wait()
    for row in range(2):
        padded[:, margin - 2 + row, :] = landing[0, row]
        padded[:, margin + span + row, :] = landing[1, row]

    def central(values, dim):
        size = values.shape[dim]
        return 0.5 * (pltpu.roll(values, size - 1, dim) - pltpu.roll(values, 1, dim))

    def plane(p, carry):
        values = padded[p]
        grad_x = 0.5 * (padded[p + 1] - padded[p - 1])
        grad_y = central(values, 0)
        grad_z = central(values, 1)
        magnitude = jnp.sqrt(grad_x * grad_x + grad_y * grad_y + grad_z * grad_z)
        inverse = -1.0 / jnp.maximum(magnitude, grad_floor)
        flow_x[p - 1] = (grad_x * inverse)[margin : margin + span]
        total = central(grad_y * inverse, 0) + central(grad_z * inverse, 1)
        partial_sum[p - 1] = total[margin : margin + span]
        return carry

    lax.fori_loop(1, xs + 3, plane, 0)


def solve_kernel(n, grad_floor, field, table, decay, scale, green, moments, mask, *rest):
    signed = grad_floor is not None
    labels = rest[0] if signed else None
    rest = rest[1:] if signed else rest
    out, waves, work, outgoing, incoming, sent, arrived, send_sem, recv_sem, wide_send, wide_recv = rest[:11]
    xs, span, length = field.shape
    wide = incoming.shape[1]
    layers = length // wide
    group = lanes // layers
    halves = length // lanes
    chunks = span // group
    parts = wide_send.shape[1]
    each = chunks // parts
    rows_each = span // parts
    step_rows = max(1, 256 // span)
    me = lax.axis_index("narrow")
    here = lax.axis_index("wide")
    mesh_ids = pl.DeviceIdType.MESH
    barrier = pltpu.get_barrier_semaphore()
    for step in range(1, n):
        pl.semaphore_signal(barrier, inc=1, device_id={"narrow": lax.rem(me + step, n)}, device_id_type=mesh_ids)

    def greet(step, carry):
        pl.semaphore_signal(barrier, inc=1, device_id={"wide": lax.rem(here + step, wide)}, device_id_type=mesh_ids)
        return carry

    lax.fori_loop(1, wide, greet, 0)

    if signed:
        pl.semaphore_wait(barrier, n - 1 + wide - 1)
        partial_sum, flow_x = rest[11:13]
        flow_stage(n, grad_floor, field, *rest[11:])

    def block_copy(turn, part, step):
        target = lax.rem(here + step, wide)
        some = pl.ds(part * each, each)
        return pltpu.make_async_remote_copy(
            src_ref=outgoing.at[turn, target, some],
            dst_ref=incoming.at[turn, here, some],
            send_sem=wide_send.at[turn, part, step],
            recv_sem=wide_recv.at[turn, part, step],
            device_id={"wide": target},
            device_id_type=mesh_ids,
        )

    def send_part(turn, part):
        def one(count, carry):
            step = 1 + lax.rem(count + wide // 2 - 2, wide - 1)
            block_copy(turn, part, step).start()
            return carry

        lax.fori_loop(1, wide, one, 0)
        some = pl.ds(part * each, each)
        incoming[turn, here, some] = outgoing[turn, here, some]

    def receive_part(turn, part):
        def one(step, carry):
            block_copy(turn, part, step).wait_recv()
            return carry

        lax.fori_loop(1, wide, one, 0)

    def finish_part(turn, part):
        def one(step, carry):
            block_copy(turn, part, step).wait_send()
            return carry

        lax.fori_loop(1, wide, one, 0)

    def transform(c, carry):
        if signed:
            planes = partial_sum[pl.ds(1 + c * step_rows, step_rows)] + 0.5 * (
                flow_x[pl.ds(2 + c * step_rows, step_rows)] - flow_x[pl.ds(c * step_rows, step_rows)]
            )
        else:
            planes = field[pl.ds(c * step_rows, step_rows)].astype(jnp.float32)
        rows = planes.reshape(step_rows * span, length)
        result = jnp.dot(rows, table[...], precision=highest, preferred_element_type=jnp.float32)
        start = pl.multiple_of(c * step_rows * span, step_rows * span)
        for h in range(halves):
            waves[h, pl.ds(start, step_rows * span), :] = result[:, h * lanes : (h + 1) * lanes]
        return carry

    lax.fori_loop(0, xs // step_rows, transform, 0)
    slot_of = lax.broadcasted_iota(jnp.int32, (xs, lanes), 1) // layers

    def split(g, carry):
        for h in range(halves):
            pieces = [waves[h, pl.ds(g * group + i, xs, stride=span), :] for i in range(group)]
            for slot in range(group):
                total = None
                for i in range(group):
                    shift = ((i - slot) * layers) % lanes
                    moved = pltpu.roll(pieces[i], shift, 1) if shift else pieces[i]
                    total = moved if total is None else jnp.where(slot_of == i, moved, total)
                outgoing[0, h * group + slot, g] = total
        return carry

    for part in range(parts):
        lax.fori_loop(part * each, (part + 1) * each, split, 0)
        if part == 0 and not signed:
            pl.semaphore_wait(barrier, n - 1 + wide - 1)
        send_part(0, part)

    r = decay[...]
    s = scale[...]

    def to_waves(c, carry):
        block = lax.dot_general(
            incoming[0, :, c].reshape(length, lanes).T, table[...], (((1,), (0,)), ((), ())), precision=highest,
            preferred_element_type=jnp.float32,
        )
        work[pl.ds(c * group, group)] = block.reshape(group, layers, length)
        return carry

    def ahead(j, v):
        v = work[j] + r * v
        work[j] = v
        return v

    v_last = jnp.zeros_like(r)
    columns = []
    for part in range(parts):
        receive_part(0, part)
        lax.fori_loop(part * each, (part + 1) * each, to_waves, 0)
        columns.append(work[part * rows_each : (part + 1) * rows_each, 0, :])
        v_last = lax.fori_loop(part * rows_each, (part + 1) * rows_each, ahead, v_last, unroll=4)
    column = jnp.concatenate(columns, axis=0)
    sent[2 * layers :, :] = jnp.dot(moments[...], column, precision=highest, preferred_element_type=jnp.float32)

    def back(i, u):
        j = span - 1 - i
        u = s * work[j] + r * u
        work[j] = u
        return u

    u_first = lax.fori_loop(0, span, back, jnp.zeros_like(r), unroll=4)
    sent[0:layers, :] = v_last
    sent[layers : 2 * layers, :] = u_first
    copies = []
    for step in range(1, n):
        copy = pltpu.make_async_remote_copy(
            src_ref=sent,
            dst_ref=arrived.at[n - 1 - step],
            send_sem=send_sem.at[step - 1],
            recv_sem=recv_sem.at[n - 1 - step],
            device_id={"narrow": lax.rem(me + step, n)},
            device_id_type=mesh_ids,
        )
        copy.start()
        copies.append(copy)
    for part in range(parts):
        finish_part(0, part)
    q = power(r, span)
    close = 1.0 / (1.0 - power(q, n))
    factor = s / (1.0 - r * r)
    tail = q * r
    edge = r - tail * q
    for copy in copies:
        copy.wait()
    stacked = jnp.concatenate([column] + [arrived[d, 2 * layers :, :] for d in range(n - 1)], axis=0)
    extra = jnp.dot(green[...], stacked, precision=highest, preferred_element_type=jnp.float32) * mask[...]
    last = [v_last] + [arrived[d, 0:layers, :] for d in range(n - 1)]
    first = [u_first] + [arrived[d, layers : 2 * layers, :] for d in range(n - 1)]
    alphas = []
    for t in range(n):
        total = last[t % n]
        for k in range(n - 2, -1, -1):
            total = last[(t - 1 - k) % n] + q * total
        alphas.append(total * close * factor)
    begin = [first[t] + alphas[t] * edge for t in range(n)]
    total = begin[0]
    for k in range(n - 2, -1, -1):
        total = begin[(1 + k) % n] + q * total
    inflow = total * close

    def add_ahead(j, p):
        work[j] = work[j] + p
        return p * r

    lax.fori_loop(0, span, add_ahead, alphas[0] * r, unroll=4)
    work[:, 0, :] = work[:, 0, :] + extra

    def add_back(i, p):
        j = span - 1 - i
        work[j] = work[j] + p
        return p * r

    def from_waves(c, carry):
        block = work[pl.ds(c * group, group)].reshape(lanes, length)
        result = lax.dot_general(
            table[...], block, (((1,), (1,)), ((), ())), precision=highest, preferred_element_type=jnp.float32
        )
        outgoing[1, :, c] = result.reshape(wide, xs, lanes)
        return carry

    p = (inflow - alphas[0] * tail) * r
    for turn in range(parts):
        part = parts - 1 - turn
        p = lax.fori_loop(turn * rows_each, (turn + 1) * rows_each, add_back, p, unroll=4)
        lax.fori_loop(part * each, (part + 1) * each, from_waves, 0)
        send_part(1, part)

    def join(g, carry):
        for h in range(halves):
            pieces = [incoming[1, h * group + slot, g] for slot in range(group)]
            for i in range(group):
                total = None
                for slot in range(group):
                    shift = ((slot - i) * layers) % lanes
                    moved = pltpu.roll(pieces[slot], shift, 1) if shift else pieces[slot]
                    total = moved if total is None else jnp.where(slot_of == slot, moved, total)
                waves[h, pl.ds(g * group + i, xs, stride=span), :] = total
        return carry

    for part in reversed(range(parts)):
        receive_part(1, part)
        lax.fori_loop(part * each, (part + 1) * each, join, 0)

    def transform_back(c, carry):
        start = pl.multiple_of(c * step_rows * span, step_rows * span)
        rows = jnp.concatenate([waves[h, pl.ds(start, step_rows * span), :] for h in range(halves)], axis=1)
        result = jnp.dot(rows, table[...], precision=highest, preferred_element_type=jnp.float32)
        result = result.reshape(step_rows, span, length)
        if signed:
            result = result * (2 * labels[pl.ds(c * step_rows, step_rows)] - 1).astype(jnp.float32)
        out[pl.ds(c * step_rows, step_rows)] = result
        return carry

    lax.fori_loop(0, xs // step_rows, transform_back, 0)
    for part in range(parts):
        finish_part(1, part)


def solve(real_field, tables, decay, scale, mask, labels=None, grad_floor=None):
    xs, span, length = real_field.shape
    n = lax.axis_size("narrow")
    wide = lax.axis_size("wide")
    layers = length // wide
    chunks = span * layers // lanes
    parts = min(8, chunks)
    rows = 2 * layers + moment_rows
    vmem = pl.BlockSpec(memory_space=pltpu.VMEM)
    args = (real_field, tables[0], decay, scale, tables[1], tables[2], mask) + (() if labels is None else (labels,))
    flow_scratch = [] if labels is None else [
        pltpu.VMEM((xs + 2, span, length), jnp.float32),
        pltpu.VMEM((xs + 2, span, length), jnp.float32),
        pltpu.VMEM((xs + 4, span + 2 * margin, length), jnp.float32),
        pltpu.VMEM((2, 2, xs + 4, length), jnp.float32),
        pltpu.VMEM((2, 2, xs + 4, length), jnp.float32),
        pltpu.SemaphoreType.DMA((4,)),
        pltpu.SemaphoreType.DMA((4,)),
    ]
    return pl.pallas_call(
        partial(solve_kernel, n, grad_floor),
        out_shape=jax.ShapeDtypeStruct(real_field.shape, jnp.float32),
        in_specs=[vmem] * len(args),
        out_specs=vmem,
        scratch_shapes=[
            pltpu.VMEM((length // lanes, xs * span, lanes), jnp.float32),
            pltpu.VMEM((span, layers, length), jnp.float32),
            pltpu.VMEM((2, wide, chunks, xs, lanes), jnp.float32),
            pltpu.VMEM((2, wide, chunks, xs, lanes), jnp.float32),
            pltpu.VMEM((rows, length), jnp.float32),
            pltpu.VMEM((n - 1, rows, length), jnp.float32),
            pltpu.SemaphoreType.DMA((n - 1,)),
            pltpu.SemaphoreType.DMA((n - 1,)),
            pltpu.SemaphoreType.DMA((2, parts, wide)),
            pltpu.SemaphoreType.DMA((2, parts, wide)),
        ]
        + flow_scratch,
        compiler_params=pltpu.CompilerParams(
            collective_id=0 if labels is None else 1, has_side_effects=True, vmem_limit_bytes=40 * 1024 * 1024
        ),
        cost_estimate=pl.CostEstimate(
            flops=8 * xs * span * length * length, bytes_accessed=8 * xs * span * length, transcendentals=0
        ),
        name="solve" if labels is None else "solve_signed",
    )(*args)


def per_device(sources, labels):
    length = sources.shape[2]
    heat_time = (length / 8.0) ** 2
    grad_floor = 0.04 / heat_time
    wide = lax.axis_size("wide")
    layers = length // wide
    place = lax.axis_index("wide")
    green, moments = column_tables(length, lax.axis_size("narrow"))
    tables = (jnp.asarray(cas_table(length)), jnp.asarray(green), jnp.asarray(moments))

    def mine(table):
        return lax.dynamic_slice_in_dim(jnp.asarray(table), place * layers, layers, axis=0)

    heat_decay = mine(decay_table(length, 1.0 / heat_time))
    line_decay = mine(decay_table(length, 0.0))
    corner = (jnp.arange(length, dtype=jnp.int32)[None, :] == 0) & (place == 0)
    norm = float(length) ** 2
    heat_field = solve(
        sources, tables, heat_decay, heat_decay * (1.0 / (heat_time * norm)),
        jnp.zeros((1, length), jnp.float32),
    )
    return solve(
        heat_field, tables, line_decay, line_decay * (-1.0 / norm), jnp.where(corner, -1.0 / norm, 0.0), labels,
        grad_floor,
    )


def solution(mesh):
    return jax.shard_map(
        per_device,
        mesh=mesh,
        in_specs=(P("wide", "narrow", None), P("wide", "narrow", None)),
        out_specs=P("wide", "narrow", None),
        check_vma=False,
    )
```
